32 devices in a mesh: slab: 8 (over y, x, core), col: 4 (over z).
Axes of the slice: x: 2, y: 2, z: 4, core: 2. Of those that a mesh axis runs over, the one named last changes fastest.
Arguments:
- rest_points: float32 [3, 8, 8, 128], P(None, 'slab', 'col'), may hold values from 0 to 8, as said below
- tile_fill: int32 [8, 8], P('slab', 'col'), may hold values from 32 to 128, as said below
- displacement: float32 [3, 8, 8, 128], P(None, 'slab', 'col'), may hold values from -0.6 to 0.6
- velocity: float32 [3, 8, 8, 128], P(None, 'slab', 'col'), may hold values from -0.6 to 0.6
- back_extension: bfloat16 [2, 8, 8, 9, 128, 128], P(None, 'slab', 'col'), may hold values from -0.59765625 to 0.59765625
Outputs:
- displacement_out: float32 [3, 8, 8, 128], P(None, 'slab', 'col')
- velocity_out: float32 [3, 8, 8, 128], P(None, 'slab', 'col')
- back_extension_out: bfloat16 [2, 8, 8, 9, 128, 128], P(None, 'slab', 'col')
The draws below stay inside these ranges and needn't reach their ends.
Inputs may be any that keep to these rules, and one draw needn't show every extreme that they name: `tile_fill`: point slots of a tile are filled from the first one; at least a quarter of the 128 slots are live. `rest_points`: the points of tile (r, c) lie in its unit box: r plus [0, 1) along the first component, c plus [0, 1) along the second, [0, 1) along the third.
All inputs are finite; a program needn't handle non-finite values.
Results may differ from the reference program's by a relative error of at most 0.0051.
Values sent between devices are 32-bit elements; how exact they have to be, the bound alone decides.
A program may use at most 128 MiB of HBM per device.

```python
import jax
import jax.numpy as jnp
from jax import lax

POINTS = 128
STEPS = 2
ROWS_ALL = 8
COLS_ALL = 8


def draw_rest_points(key, part):
    spread = jax.random.uniform(key, (3, ROWS_ALL, COLS_ALL, POINTS), jnp.float32)
    row_base = jnp.arange(ROWS_ALL, dtype=jnp.float32)[:, None, None]
    col_base = jnp.arange(COLS_ALL, dtype=jnp.float32)[None, :, None]
    return jnp.stack([row_base + spread[0], col_base + spread[1], spread[2]], 0)


def draw_tile_fill(key, part):
    counts = jax.random.randint(jax.random.fold_in(key, 7), (ROWS_ALL, COLS_ALL), POINTS // 4, POINTS + POINTS // 4 + 1)
    return jnp.minimum(counts, POINTS).astype(jnp.int32)


def levels(own_key, shape, split, smallest, high):
    def one(axis_at, blocks):
        steps = jax.random.uniform(jax.random.fold_in(jax.random.fold_in(own_key, 6), axis_at), (blocks,), jnp.float32, smallest / len(split), high / len(split))
        return jnp.repeat(jnp.exp(steps), shape[axis_at] // blocks).reshape((-1,) + (1,) * (len(shape) - axis_at - 1))

    loudness = one(*split[0])
    for cut in split[1:]:
        loudness = loudness * one(*cut)
    return loudness


def gaussian(rng, extent, width, bound, pieces=(), kind=jnp.bfloat16):
    gain = levels(rng, extent, pieces, -0.22, 0.18) if pieces else 1.0
    values = jax.random.normal(rng, extent, jnp.float32) * width * gain
    return jnp.minimum(jnp.maximum(values, -bound), bound).astype(kind)


def setup_inputs(seed: int = 0) -> dict:
    key_of = jax.random.split(jax.random.key(seed), 6)
    rest_points = draw_rest_points(jax.random.fold_in(key_of[5], 71), 0)
    tile_fill = draw_tile_fill(jax.random.fold_in(key_of[5], 71), 0)
    displacement = gaussian(key_of[2], (3, ROWS_ALL, COLS_ALL, POINTS), 0.1, 0.6, ((1, 8), (2, 4)), jnp.float32)
    velocity = gaussian(key_of[3], (3, ROWS_ALL, COLS_ALL, POINTS), 0.1, 0.6, ((1, 8), (2, 4)), jnp.float32)
    back_extension = gaussian(key_of[4], (2, ROWS_ALL, COLS_ALL, 9, POINTS, POINTS), 0.1, 0.59765625, ((1, 8), (2, 4)))
    return dict(rest_points=rest_points, tile_fill=tile_fill, displacement=displacement, velocity=velocity, back_extension=back_extension)


stencil_offsets = [(-1, -1), (-1, 0), (-1, 1), (0, -1), (0, 0), (0, 1), (1, -1), (1, 0), (1, 1)]

def pad_tiles(values, first):
    widths = [(0, 0)] * values.ndim
    widths[first] = (1, 1)
    widths[first + 1] = (1, 1)
    return jnp.pad(values, widths)

def pair_geometry(rest_halo, alive_halo, rows, cols, row_shift, col_shift):
    home_side = rest_halo[:, 1:1 + rows, 1:1 + cols, :, None]
    far_side = rest_halo[:, 1 + row_shift:1 + row_shift + rows, 1 + col_shift:1 + col_shift + cols, None, :]
    bond = far_side - home_side
    length = jnp.sqrt(lax.optimization_barrier(jnp.sum(bond * bond, axis=0)))
    closeness = jnp.maximum(1.0 - length, 0.0)
    weight = closeness * closeness * alive_halo[1:1 + rows, 1:1 + cols, :, None]
    weight = weight * alive_halo[1 + row_shift:1 + row_shift + rows, 1 + col_shift:1 + col_shift + cols, None, :]
    if row_shift == 0 and col_shift == 0:
        weight = weight * (1.0 - jnp.eye(weight.shape[-1], dtype=jnp.float32))
    return (length, weight)

def deformed(place_halo, length, rows, cols, row_shift, col_shift):
    home_side = place_halo[:, 1:1 + rows, 1:1 + cols, :, None]
    far_side = place_halo[:, 1 + row_shift:1 + row_shift + rows, 1 + col_shift:1 + col_shift + cols, None, :]
    separation = far_side - home_side
    squared = lax.optimization_barrier(jnp.sum(separation * separation, axis=0))
    stretch = jnp.sqrt(squared) - length
    bearing = separation * jax.lax.rsqrt(squared + 0.01)
    return (stretch, bearing)

def reference(rest_points, tile_fill, displacement, velocity, back_extension):
    rows, cols, points = (rest_points.shape[1], rest_points.shape[2], rest_points.shape[3])
    alive = (jnp.arange(points, dtype=jnp.int32)[None, None, :] < tile_fill[:, :, None]).astype(jnp.float32)
    rest_halo = pad_tiles(rest_points, 1)
    alive_halo = pad_tiles(alive, 0)
    geometry = [pair_geometry(rest_halo, alive_halo, rows, cols, rs, cs) for rs, cs in stencil_offsets]
    volume = jnp.zeros((rows, cols, points), jnp.float32)
    for length, weight in geometry:
        volume = volume + lax.optimization_barrier(jnp.sum(weight * length * length, axis=-1))
    volume = jnp.maximum(volume, 1.0)
    history = back_extension
    for step_index in range(STEPS):
        place_halo = rest_halo + pad_tiles(displacement, 1)
        shapes = [deformed(place_halo, geometry[index][0], rows, cols, rs, cs) for index, (rs, cs) in enumerate(stencil_offsets)]
        dilatation = jnp.zeros((rows, cols, points), jnp.float32)
        for index in range(9):
            length, weight = geometry[index]
            dilatation = dilatation + lax.optimization_barrier(jnp.sum(weight * length * shapes[index][0], axis=-1))
        dilatation = 3.0 * dilatation / volume
        forces, first_states, second_states = ([], [], [])
        for index in range(9):
            length, weight = geometry[index]
            deviator = shapes[index][0] - dilatation[..., None] * length / 3.0
            back_one = 0.6 * history[0, :, :, index].astype(jnp.float32) + 0.4 * deviator
            back_two = 0.95 * history[1, :, :, index].astype(jnp.float32) + 0.05 * deviator
            bond_force = 3.0 * dilatation[..., None] * weight * length / volume[..., None]
            bond_force = bond_force + 7.5 * weight / volume[..., None] * (0.4 * deviator + 0.35 * (deviator - back_one) + 0.25 * (deviator - back_two))
            forces.append(bond_force)
            first_states.append(back_one)
            second_states.append(back_two)
        history = jnp.stack([jnp.stack(first_states, 2), jnp.stack(second_states, 2)], 0).astype(jnp.bfloat16)
        force_halo = pad_tiles(jnp.stack(forces, 0), 1)
        total_force = jnp.zeros((3, rows, cols, points), jnp.float32)
        for index, (rs, cs) in enumerate(stencil_offsets):
            reverse = force_halo[8 - index, 1 + rs:1 + rs + rows, 1 + cs:1 + cs + cols]
            reverse = jnp.swapaxes(reverse, -1, -2)
            total_force = total_force + lax.optimization_barrier(jnp.sum((forces[index] + reverse)[None] * shapes[index][1], axis=-1))
        velocity = velocity + 0.2 * total_force
        displacement = displacement + 0.2 * velocity
    return (displacement, velocity, history)
```

```python
import functools

import jax
import jax.numpy as jnp
from jax import lax
from jax.experimental import pallas as pl
from jax.experimental.pallas import tpu as pltpu
from jax.sharding import PartitionSpec as P

MESH = pl.DeviceIdType.MESH
STENCIL = [(-1, -1), (-1, 0), (-1, 1), (0, -1), (0, 0), (0, 1), (1, -1), (1, 0), (1, 1)]
NEAR = [(dr, dc) for dr in (-1, 0, 1) for dc in (-1, 0, 1) if (dr, dc) != (0, 0)]
WIDE = [(dr, dc) for dr in (-2, -1, 0, 1, 2) for dc in (-1, 0, 1) if (dr, dc) != (0, 0)]
CHUNK = 16
TINY = 1e-30


def kernel(
    slabs, sections, tiles, points,
    rest_ref, fill_ref, disp_ref, vel_ref, hist_hbm,
    disp_out, vel_out, hist_out,
    hist, halo, place, pulls, last_pulls, wide_in, near_in,
    length_s, weight_s, stretch_s, pull_s,
    home_rest, home_place, sums, theta, inverse_mass, partial,
    hist_in_sem, hist_out_sem, send_a, recv_a, send_b, recv_b, send_c, recv_c,
):
    r, c = lax.axis_index("slab"), lax.axis_index("col")
    chunks = points // CHUNK
    f32 = jnp.float32

    def inside(dr, dc):
        row, col = r + dr, c + dc
        return (row >= 0) & (row < slabs) & (col >= 0) & (col < sections)

    load_hist = pltpu.make_async_copy(hist_hbm, hist, hist_in_sem)
    load_hist.start()

    halo[...] = jnp.zeros_like(halo)
    wide_in[...] = jnp.zeros_like(wide_in)
    near_in[...] = jnp.zeros_like(near_in)

    barrier = pltpu.get_barrier_semaphore()
    for dr, dc in WIDE:
        @pl.when(inside(dr, dc))
        def _():
            pl.semaphore_signal(barrier, inc=1, device_id=(r + dr, c + dc), device_id_type=MESH)

    lane = lax.broadcasted_iota(jnp.int32, (1, points), 1)
    for t in range(tiles):
        for i in range(3):
            halo[1, 1 + t, i : i + 1, :] = rest_ref[i, 0, t : t + 1, :]
            halo[1, 1 + t, 4 + i : 5 + i, :] = disp_ref[i, 0, t : t + 1, :]
            halo[1, 1 + t, 8 + i : 9 + i, :] = vel_ref[i, 0, t : t + 1, :]
        halo[1, 1 + t, 3:4, :] = (lane < fill_ref[0:1, t : t + 1]).astype(f32)

    low_rows = jnp.minimum(r, 2)
    high_rows = jnp.minimum(slabs - 1 - r, 2)
    side_cols = jnp.minimum(c, 1) + jnp.minimum(sections - 1 - c, 1)
    pl.semaphore_wait(barrier, (low_rows + high_rows + 1) * (side_cols + 1) - 1)

    def halo_copy(n):
        dr, dc = NEAR[n]
        src, dst, count = {0: (1, 1, tiles), 1: (tiles, 0, 1), -1: (1, tiles + 1, 1)}[dc]
        return pltpu.make_async_remote_copy(
            src_ref=halo.at[1, pl.ds(src, count)],
            dst_ref=halo.at[1 - dr, pl.ds(dst, count)],
            send_sem=send_a.at[n], recv_sem=recv_a.at[n],
            device_id=(r + dr, c + dc), device_id_type=MESH,
        )

    def wide_copy(n):
        dr, dc = WIDE[n]
        row, rows = max(0, dr), min(2, 2 + dr) - max(0, dr) + 1
        col = max(0, tiles * dc)
        cols = min(tiles + 1, tiles + 1 + tiles * dc) - col + 1
        return pltpu.make_async_remote_copy(
            src_ref=pulls.at[pl.ds(row, rows), pl.ds(col, cols)],
            dst_ref=wide_in.at[n, pl.ds(row - dr, rows), pl.ds(col - tiles * dc, cols)],
            send_sem=send_b.at[n], recv_sem=recv_b.at[n],
            device_id=(r + dr, c + dc), device_id_type=MESH,
        )

    def near_copy(n):
        dr, dc = NEAR[n]
        src, dst, count = {0: (1, 0, tiles), 1: (tiles + 1, 0, 1), -1: (0, tiles - 1, 1)}[dc]
        return pltpu.make_async_remote_copy(
            src_ref=last_pulls.at[1 + dr, pl.ds(src, count)],
            dst_ref=near_in.at[n, pl.ds(dst, count)],
            send_sem=send_c.at[n], recv_sem=recv_c.at[n],
            device_id=(r + dr, c + dc), device_id_type=MESH,
        )

    def start_all(peers, copy):
        for n, (dr, dc) in enumerate(peers):
            @pl.when(inside(dr, dc))
            def _():
                copy(n).start()

    def receive_all(peers, copy):
        for n, (dr, dc) in enumerate(peers):
            @pl.when(inside(-dr, -dc))
            def _():
                copy(n).wait_recv()

    def sent_all(peers, copy):
        for n, (dr, dc) in enumerate(peers):
            @pl.when(inside(dr, dc))
            def _():
                copy(n).wait_send()

    def over_lanes(rows):
        turned = rows.T
        return [jnp.broadcast_to(turned[:, i : i + 1], (points, points)) for i in range(3)]

    start_all(NEAR, halo_copy)
    for t in range(tiles):
        own = halo[1, 1 + t, 0:8, :]
        for i, wide in enumerate(over_lanes(own)):
            home_rest[t, i] = wide
        for i, wide in enumerate(over_lanes(own + pltpu.roll(own, 4, 0))):
            home_place[t, i] = wide
    receive_all(NEAR, halo_copy)
    place[...] = halo[:, :, 0:4, :] + halo[:, :, 4:8, :]

    def measure(first):
        for t in range(tiles):
            def body(n, carry):
                start = pl.multiple_of(n * CHUNK, CHUNK)
                at = pl.ds(start, CHUNK)
                volume = jnp.zeros((CHUNK, points), f32)
                spread = jnp.zeros((CHUNK, points), f32)
                for k, (dr, dc) in enumerate(STENCIL):
                    far = (1 + dr, 1 + t + dc)
                    if first:
                        bond = [halo[far[0], far[1], i : i + 1, :] - home_rest[t, i, at, :] for i in range(3)]
                        square = bond[0] * bond[0] + bond[1] * bond[1] + bond[2] * bond[2]
                        length = square * lax.rsqrt(jnp.maximum(square, TINY))
                        close = jnp.maximum(1.0 - length, 0.0)
                        weight = close * close * halo[far[0], far[1], 3:4, :]
                        if (dr, dc) == (0, 0):
                            a = lax.broadcasted_iota(jnp.int32, (CHUNK, points), 0) + start
                            b = lax.broadcasted_iota(jnp.int32, (CHUNK, points), 1)
                            weight = jnp.where(a == b, 0.0, weight)
                        length_s[t, k, at, :] = length
                        weight_s[t, k, at, :] = weight
                    else:
                        length = length_s[t, k, at, :]
                        weight = weight_s[t, k, at, :]
                    reach = weight * length
                    if first:
                        volume = volume + reach * length
                    apart = [place[far[0], far[1], i : i + 1, :] - home_place[t, i, at, :] for i in range(3)]
                    square = apart[0] * apart[0] + apart[1] * apart[1] + apart[2] * apart[2]
                    stretch = square * lax.rsqrt(jnp.maximum(square, TINY)) - length
                    stretch_s[t, k, at, :] = stretch
                    pull_s[t, k, at, :] = weight * lax.rsqrt(square + 0.01)
                    spread = spread + reach * stretch
                sums[0, t, at, :] = spread
                if first:
                    sums[1, t, at, :] = volume
                return carry
            lax.fori_loop(0, chunks, body, 0)
        for t in range(tiles):
            if first:
                volume = jnp.sum(sums[1, t], axis=-1, keepdims=True)
                a = lax.broadcasted_iota(jnp.int32, (points, 1), 0)
                inverse = jnp.where(a < fill_ref[0:1, t : t + 1], 1.0 / jnp.maximum(volume, 1.0), 0.0)
                inverse_mass[t] = jnp.broadcast_to(inverse, (points, points))
            spread = jnp.sum(sums[0, t], axis=-1, keepdims=True)
            theta[t] = jnp.broadcast_to(spread, (points, points)) * inverse_mass[t]

    def pull(result):
        for t in range(tiles):
            def body(n, carry):
                at = pl.ds(pl.multiple_of(n * CHUNK, CHUNK), CHUNK)
                scaled = theta[t, at, :] * 2.64375
                inverse = inverse_mass[t, at, :]
                direct = [jnp.zeros((CHUNK, points), f32)] * 3
                for k, (dr, dc) in enumerate(STENCIL):
                    one = hist[0, 0, t, k, at, :].astype(f32)
                    two = hist[1, 0, t, k, at, :].astype(f32)
                    force = scaled * length_s[t, k, at, :] + 6.35625 * stretch_s[t, k, at, :]
                    force = force - 1.575 * one - 1.78125 * two
                    force = force * inverse * pull_s[t, k, at, :]
                    for i in range(3):
                        part = force * (place[1 + dr, 1 + t + dc, i : i + 1, :] - home_place[t, i, at, :])
                        direct[i] = direct[i] + part
                        folded = part[0:8]
                        for q in range(8, CHUNK, 8):
                            folded = folded + part[q : q + 8]
                        partial[t, n, k, i] = folded
                for i in range(3):
                    sums[i, t, at, :] = direct[i]
                return carry
            lax.fori_loop(0, chunks, body, 0)
        ones = jnp.ones((8, points), f32)
        for row in range(3):
            for col in range(tiles + 2):
                for i in range(3):
                    total = None
                    for t in range(tiles):
                        for k, (dr, dc) in enumerate(STENCIL):
                            if (1 + dr, 1 + t + dc) == (row, col):
                                piece = jnp.sum(partial[t, :, k, i], axis=0)
                                total = piece if total is None else total + piece
                    total = -jnp.sum(total, axis=0, keepdims=True)
                    if row == 1 and 1 <= col <= tiles:
                        direct = lax.dot_general(
                            ones, sums[i, col - 1], (((1,), (1,)), ((), ())),
                            precision=lax.Precision.HIGHEST, preferred_element_type=f32,
                        )
                        total = total + direct[0:1]
                    result[row, col, i : i + 1, :] = total
                result[row, col, 3:4, :] = jnp.zeros((1, points), f32)

    def relax(t):
        def body(n, carry):
            at = pl.ds(pl.multiple_of(n * CHUNK, CHUNK), CHUNK)
            third = theta[t, at, :]
            for k in range(9):
                deviator = stretch_s[t, k, at, :] - third * length_s[t, k, at, :]
                for j, decay in enumerate((0.6, 0.95)):
                    back = decay * hist[j, 0, t, k, at, :].astype(f32) + (1.0 - decay) * deviator
                    hist[j, 0, t, k, at, :] = back.astype(hist.dtype)
            return carry
        lax.fori_loop(0, chunks, body, 0)

    measure(True)
    load_hist.wait()
    pull(pulls)
    start_all(WIDE, wide_copy)
    for t in range(tiles):
        relax(t)
    receive_all(WIDE, wide_copy)

    force = pulls[...]
    for n in range(len(WIDE)):
        force = force + wide_in[n]
    speed = halo[:, :, 8:12, :] + 0.2 * force
    moved = halo[:, :, 4:8, :] + 0.2 * speed
    place[...] = halo[:, :, 0:4, :] + moved
    speed = speed[1, 1 : 1 + tiles]
    moved = moved[1, 1 : 1 + tiles]
    for t in range(tiles):
        own = jnp.concatenate([place[1, 1 + t], jnp.zeros((4, points), f32)], axis=0)
        for i, wide in enumerate(over_lanes(own)):
            home_place[t, i] = wide

    measure(False)
    pull(last_pulls)
    start_all(NEAR, near_copy)
    stores = []
    for t in range(tiles):
        relax(t)
        for j in range(2):
            store = pltpu.make_async_copy(hist.at[j, 0, t], hist_out.at[j, 0, t], hist_out_sem.at[j, t])
            store.start()
            stores.append(store)
    receive_all(NEAR, near_copy)

    force = last_pulls[1, 1 : 1 + tiles]
    for n in range(len(NEAR)):
        force = force + near_in[n]
    speed = speed + 0.2 * force
    moved = moved + 0.2 * speed
    for t in range(tiles):
        for i in range(3):
            disp_out[i, 0, t : t + 1, :] = moved[t, i : i + 1, :]
            vel_out[i, 0, t : t + 1, :] = speed[t, i : i + 1, :]
    sent_all(NEAR, halo_copy)
    sent_all(WIDE, wide_copy)
    sent_all(NEAR, near_copy)
    for store in stores:
        store.wait()


def per_device(slabs, sections, rest_points, tile_fill, displacement, velocity, back_extension):
    _, rows, tiles, points = rest_points.shape
    assert rows == 1 and tiles >= 2
    f32 = jnp.float32
    vmem = pl.BlockSpec(memory_space=pltpu.VMEM)
    anywhere = pl.BlockSpec(memory_space=pl.ANY)
    bonds = (tiles, 9, points, points)
    dma = pltpu.SemaphoreType.DMA
    return pl.pallas_call(
        functools.partial(kernel, slabs, sections, tiles, points),
        out_shape=(
            jax.ShapeDtypeStruct(displacement.shape, f32),
            jax.ShapeDtypeStruct(velocity.shape, f32),
            jax.ShapeDtypeStruct(back_extension.shape, back_extension.dtype),
        ),
        in_specs=[vmem, vmem, vmem, vmem, anywhere],
        out_specs=(vmem, vmem, anywhere),
        scratch_shapes=[
            pltpu.VMEM(back_extension.shape, back_extension.dtype),
            pltpu.VMEM((3, tiles + 2, 16, points), f32),
            pltpu.VMEM((3, tiles + 2, 4, points), f32),
            pltpu.VMEM((3, tiles + 2, 4, points), f32),
            pltpu.VMEM((3, tiles + 2, 4, points), f32),
            pltpu.VMEM((len(WIDE), 3, tiles + 2, 4, points), f32),
            pltpu.VMEM((len(NEAR), tiles, 4, points), f32),
            pltpu.VMEM(bonds, f32),
            pltpu.VMEM(bonds, f32),
            pltpu.VMEM(bonds, f32),
            pltpu.VMEM(bonds, f32),
            pltpu.VMEM((tiles, 3, points, points), f32),
            pltpu.VMEM((tiles, 3, points, points), f32),
            pltpu.VMEM((3, tiles, points, points), f32),
            pltpu.VMEM((tiles, points, points), f32),
            pltpu.VMEM((tiles, points, points), f32),
            pltpu.VMEM((tiles, points // CHUNK, 9, 3, 8, points), f32),
            dma,
            dma((2, tiles)),
            dma((len(NEAR),)), dma((len(NEAR),)),
            dma((len(WIDE),)), dma((len(WIDE),)),
            dma((len(NEAR),)), dma((len(NEAR),)),
        ],
        compiler_params=pltpu.CompilerParams(
            collective_id=0, has_side_effects=True, vmem_limit_bytes=48 * 1024 * 1024
        ),
    )(rest_points, tile_fill, displacement, velocity, back_extension)


def solution(mesh):
    tiles = P(None, "slab", "col", None)
    states = P(None, "slab", "col", None, None, None)
    return jax.shard_map(
        functools.partial(per_device, mesh.shape["slab"], mesh.shape["col"]),
        mesh=mesh,
        in_specs=(tiles, P("slab", "col"), tiles, tiles, states),
        out_specs=(tiles, tiles, states),
        check_vma=False,
    )
```
